32 devices in a mesh: blk: 8 (over y, x, core), grp: 4 (over z).
Axes of the slice: x: 2, y: 2, z: 4, core: 2. Of those that a mesh axis runs over, the one named last changes fastest.
Arguments:
- sky_map: bfloat16 [256, 262144], P(None, ('blk', 'grp')), may hold values from -128 to 128
- fg_templates: bfloat16 [256, 16], replicated, may hold values from -0.375 to 0.375
- cycle_len: int32 [128], P(('blk', 'grp')), may hold values from 512 to 2048, as said below
- beam_profile: float32 [8, 1024], replicated, may hold values from 0.2 to 2
- beam_index: int32 [256], P('blk'), may hold values from 0 to 7
Outputs:
- filtered: float32 [1024, 256, 2, 1024], P(None, 'blk', None, 'grp')
The draws below stay inside these ranges and needn't reach their ends.
Inputs may be any that keep to these rules, and one draw needn't show every extreme that they name: `cycle_len`: some cycle has exactly 2048 pixels.
All inputs are finite; a program needn't handle non-finite values.
Results may differ from the reference program's by a relative error of at most 0.0064.
Values may be sent and summed in bfloat16 or wider, within the bound.
A program may use at most 192 MiB of HBM per device.

```python
import math
import jax
import jax.numpy as jnp
from jax import lax

NCH = 256
NMODE = 16
RPIX = 2048
L = 1024
NPROF = 8
MW = 1024
NRING = 128


def draw_sky_map(key, part):
    keys = jax.random.split(key, 3)
    cycle_scale = jnp.exp(jax.random.uniform(keys[0], (NRING,), jnp.float32, jnp.log(0.4), jnp.log(4.0)))
    chan_scale = jnp.exp(jax.random.uniform(keys[1], (NCH,), jnp.float32, jnp.log(0.5), jnp.log(2.0)))
    base = jnp.clip(jax.random.normal(keys[2], (NCH, NRING, RPIX), jnp.float32), -4.0, 4.0)
    values = base * chan_scale[:, None, None] * cycle_scale[None, :, None]
    return values.reshape(NCH, NRING * RPIX).astype(jnp.bfloat16)


def draw_cycle_len(key, part):
    first, second = jax.random.split(key)
    lengths = jax.random.randint(first, (NRING,), RPIX // 4, RPIX + 1, jnp.int32)
    spot = jax.random.randint(second, (), 0, NRING, jnp.int32)
    return lengths.at[spot].set(RPIX)


def plant(values, stream_key, smallest, high):
    dims = values.shape
    index_at = [jax.random.randint(jax.random.fold_in(stream_key, axis), (), 0, dims[axis]) for axis in range(len(dims))]
    values = values.at[tuple(index_at)].set(smallest)
    longest = dims.index(max(dims))
    index_at[longest] = (index_at[longest] + 1) % dims[longest]
    return values.at[tuple(index_at)].set(high)


def normal_values(own_key, dims, width, most, kind=jnp.bfloat16):
    drawn = width * jax.random.normal(own_key, dims, jnp.float32)
    return jnp.clip(drawn, min=-most, max=most).astype(kind)


def setup_inputs(seed: int = 0) -> dict:
    arg_keys = jax.random.split(jax.random.key(seed), 6)
    sky_map = draw_sky_map(jax.random.fold_in(arg_keys[5], 71), 0)
    fg_templates = normal_values(arg_keys[1], (NCH, NMODE), NCH ** -0.5, 0.375)
    cycle_len = draw_cycle_len(jax.random.fold_in(arg_keys[5], 71), 0)
    beam_profile = jnp.clip(jnp.exp(jax.random.uniform(arg_keys[3], (NPROF, L), jnp.float32, math.log(0.2), math.log(2.0))), 0.2, 2.0)
    beam_index = plant(jax.random.randint(arg_keys[4], (NCH,), 0, NPROF), jax.random.fold_in(arg_keys[4], 1), 0, NPROF - 1).astype(jnp.int32)
    return {"sky_map": sky_map, "fg_templates": fg_templates, "cycle_len": cycle_len, "beam_profile": beam_profile, "beam_index": beam_index}


def cycle_table(length, m_width):
    slots = jnp.arange(RPIX, dtype=jnp.int32)
    orders = jnp.arange(m_width, dtype=jnp.int32)
    phase = orders[None, :] * (2 * slots[:, None] + 1) % (2 * length)
    angle = jnp.pi * phase.astype(jnp.float32) / length.astype(jnp.float32)
    weight = jnp.where(slots < length, 1.0, 0.0).astype(jnp.float32) * lax.rsqrt(length.astype(jnp.float32))
    table = jnp.concatenate([jnp.cos(angle), -jnp.sin(angle)], axis=1) * weight[:, None]
    return table.astype(jnp.bfloat16)

def theta_table(cycle_ids, n_cycle):
    degrees = jnp.arange(L, dtype=jnp.int32)
    odd = 2 * cycle_ids + 1
    phase = degrees[:, None] * odd[None, :] % (4 * n_cycle)
    angle = jnp.pi * phase.astype(jnp.float32) / (2.0 * n_cycle)
    weight = jnp.sin(jnp.pi * odd.astype(jnp.float32) / (2.0 * n_cycle)) * (2.0 / jnp.sqrt(jnp.float32(n_cycle)))
    return (jnp.cos(angle) * weight[None, :]).astype(jnp.bfloat16)

def reference(sky_map, fg_templates, cycle_len, beam_profile, beam_index):
    slots = jnp.arange(RPIX, dtype=jnp.int32)
    valid = (slots[None, :] < cycle_len[:, None]).reshape(-1)
    masked = jnp.where(valid[None, :], sky_map, jnp.zeros((), jnp.bfloat16))
    mode_amps = jnp.dot(fg_templates.T.astype(jnp.float32), masked.astype(jnp.float32), preferred_element_type=jnp.float32).astype(jnp.bfloat16)
    gram_sum = jnp.dot(mode_amps.astype(jnp.float32), mode_amps.T.astype(jnp.float32), preferred_element_type=jnp.float32)
    cross_sum = lax.dot_general(mode_amps.astype(jnp.float32), masked.astype(jnp.float32), (((1,), (1,)), ((), ())), preferred_element_type=jnp.float32)
    coef = jnp.linalg.solve(gram_sum, cross_sum)
    amps_wide = mode_amps.astype(jnp.float32)

    def per_cycle(inputs):
        index, length = inputs
        start = (index * RPIX).astype(jnp.int32)
        block = lax.dynamic_slice_in_dim(masked, start, RPIX, 1)
        modes = lax.dynamic_slice_in_dim(amps_wide, start, RPIX, 1)
        cleaned = (block.astype(jnp.float32) - jnp.dot(coef.T, modes, precision=lax.Precision.HIGHEST)).astype(jnp.bfloat16)
        return jnp.dot(cleaned.astype(jnp.float32), cycle_table(length, MW).astype(jnp.float32), preferred_element_type=jnp.float32).astype(jnp.bfloat16)
    fourier = lax.map(per_cycle, (jnp.arange(NRING, dtype=jnp.int32), cycle_len))
    theta_tab = theta_table(jnp.arange(NRING, dtype=jnp.int32), NRING)
    harmonic = jnp.dot(theta_tab.astype(jnp.float32), fourier.reshape(NRING, -1).astype(jnp.float32), preferred_element_type=jnp.float32)
    harmonic = harmonic.reshape(L, NCH, 2, MW)
    profiles = beam_profile[beam_index]
    shaped = harmonic * profiles.T[:, :, None, None]
    mweight = 0.25 + jnp.arange(MW, dtype=jnp.int32).astype(jnp.float32) / MW
    weighted = shaped * mweight[None, None, None, :]
    power = lax.optimization_barrier(jnp.sum(weighted * weighted, axis=(0, 2, 3)))
    return weighted * lax.rsqrt(power / (2.0 * L * MW) + 1e-06)[None, :, None, None]
```

```python
import functools
import math

import jax
import jax.numpy as jnp
from jax import lax
from jax.experimental import pallas as pl
from jax.experimental.pallas import tpu as pltpu
from jax.sharding import PartitionSpec as P

RPIX = 2048
L = 1024
M_DEV = 256
LANES = 128
FINE = 32
DEPTH = 512
VMEM = 56 * 1024 * 1024
MESH = pl.DeviceIdType.MESH


def cos_sin(phase, half):
    turns = jnp.floor(phase * (0.5 / half))
    rest = phase - turns * (2.0 * half)
    y = (rest - half) * (0.5 * math.pi / half)
    z = y * y
    s = jnp.full_like(z, -1.0 / math.factorial(11))
    for k, sign in ((9, 1), (7, -1), (5, 1), (3, -1), (1, 1)):
        s = s * z + sign / math.factorial(k)
    s = s * y
    c = jnp.full_like(z, 1.0 / math.factorial(12))
    for k, sign in ((10, -1), (8, 1), (6, -1), (4, 1), (2, -1), (0, 1)):
        c = c * z + sign / math.factorial(k)
    return 2.0 * s * s - 1.0, -2.0 * s * c


def whole_numbers(count, step=1, start=0):
    return (start + step * jnp.arange(count, dtype=jnp.int32)).astype(jnp.float32)


def cycle_factors(cycle_len, m_width):
    half = cycle_len.astype(jnp.float32)[:, None, None]
    orders = whole_numbers(m_width)[None, None, :]
    fine = whole_numbers(FINE, 2, 1)[None, :, None] * orders
    coarse = whole_numbers(RPIX // FINE, 2 * FINE)[None, :, None] * orders
    weight = lax.rsqrt(half)
    ac, as_ = cos_sin(fine, half)
    bc, bs = cos_sin(coarse, half)
    return ac * weight, as_ * weight, bc, bs


def theta_table(n_cycle):
    odd = whole_numbers(n_cycle, 2, 1)
    half = jnp.float32(2 * n_cycle)
    cosine, _ = cos_sin(whole_numbers(L)[:, None] * odd[None, :], half)
    weight = jnp.sin(jnp.pi * odd / (2.0 * n_cycle)) * (2.0 / jnp.sqrt(jnp.float32(n_cycle)))
    return (cosine * weight[None, :]).astype(jnp.bfloat16)


def sum_kernel(n_blk, n_grp, part_ref, out_ref, got_blk, got_grp, mid, ssem, rsem, ssem2, rsem2):
    blk, grp = lax.axis_index("blk"), lax.axis_index("grp")
    barrier = pltpu.get_barrier_semaphore()
    for s in range(1, n_blk):
        peer = lax.rem(blk + s, n_blk)
        pl.semaphore_signal(barrier, inc=1, device_id=(peer, grp), device_id_type=MESH)
    for s in range(1, n_grp):
        peer = lax.rem(grp + s, n_grp)
        pl.semaphore_signal(barrier, inc=1, device_id=(blk, peer), device_id_type=MESH)
    pl.semaphore_wait(barrier, n_blk - 1 + n_grp - 1)
    copies = []
    for s in range(1, n_blk):
        copies.append(
            pltpu.make_async_remote_copy(
                src_ref=part_ref,
                dst_ref=got_blk.at[s],
                send_sem=ssem.at[s],
                recv_sem=rsem.at[s],
                device_id=(lax.rem(blk + s, n_blk), grp),
                device_id_type=MESH,
            )
        )
        copies[-1].start()
    got_blk[0] = part_ref[...]
    for copy in copies:
        copy.wait()
    total = jnp.zeros(part_ref.shape, jnp.float32)
    for b in range(n_blk):
        total = total + got_blk[lax.rem(blk - b + n_blk, n_blk)]
    mid[...] = total
    copies = []
    for s in range(1, n_grp):
        copies.append(
            pltpu.make_async_remote_copy(
                src_ref=mid,
                dst_ref=got_grp.at[s],
                send_sem=ssem2.at[s],
                recv_sem=rsem2.at[s],
                device_id=(blk, lax.rem(grp + s, n_grp)),
                device_id_type=MESH,
            )
        )
        copies[-1].start()
    got_grp[0] = total
    for copy in copies:
        copy.wait()
    total = jnp.zeros(part_ref.shape, jnp.float32)
    for g in range(n_grp):
        total = total + got_grp[lax.rem(grp - g + n_grp, n_grp)]
    out_ref[...] = total


def sum_all(part, n_blk, n_grp):
    shape = part.shape
    vmem = pl.BlockSpec(memory_space=pltpu.VMEM)
    return pl.pallas_call(
        functools.partial(sum_kernel, n_blk, n_grp),
        out_shape=jax.ShapeDtypeStruct(shape, jnp.float32),
        in_specs=[vmem],
        out_specs=vmem,
        scratch_shapes=[
            pltpu.VMEM((n_blk,) + shape, jnp.float32),
            pltpu.VMEM((n_grp,) + shape, jnp.float32),
            pltpu.VMEM(shape, jnp.float32),
            pltpu.SemaphoreType.DMA((n_blk,)),
            pltpu.SemaphoreType.DMA((n_blk,)),
            pltpu.SemaphoreType.DMA((n_grp,)),
            pltpu.SemaphoreType.DMA((n_grp,)),
        ],
        compiler_params=pltpu.CompilerParams(
            collective_id=0, has_side_effects=True, vmem_limit_bytes=16 * 1024 * 1024
        ),
        name="sum_all",
    )(part)


def fourier_kernel(n_blk, n_grp, x_ref, ac_ref, as_ref, bc_ref, bs_ref, out_ref, tab, acc):
    k = pl.program_id(1)
    m_width = ac_ref.shape[2]
    chan = out_ref.shape[4]

    def column(t, carry):
        at = pl.multiple_of(t * LANES, LANES)
        ac = ac_ref[0, :, pl.ds(at, LANES)]
        as_ = as_ref[0, :, pl.ds(at, LANES)]
        for i in range(DEPTH // FINE):
            bc = bc_ref[0, pl.ds(i, 1), pl.ds(at, LANES)]
            bs = bs_ref[0, pl.ds(i, 1), pl.ds(at, LANES)]
            rows = pl.ds(i * FINE, FINE)
            tab[rows, pl.ds(at, LANES)] = (ac * bc - as_ * bs).astype(jnp.bfloat16)
            low = pl.multiple_of(m_width + at, LANES)
            tab[rows, pl.ds(low, LANES)] = -(as_ * bc + ac * bs).astype(jnp.bfloat16)
        return carry

    lax.fori_loop(0, m_width // LANES, column, 0)

    @pl.when(k == 0)
    def _():
        acc[...] = jnp.zeros_like(acc)

    for t in range(2 * m_width // 512):
        cols = pl.ds(t * 512, 512)
        acc[:, cols] += jnp.dot(x_ref[...], tab[:, cols], preferred_element_type=jnp.float32)

    @pl.when(k == pl.num_programs(1) - 1)
    def _():
        tiles = M_DEV // LANES
        for g in range(n_grp):
            for mt in range(tiles):
                for p in range(2):
                    at = p * m_width + g * M_DEV + mt * LANES
                    for b in range(n_blk):
                        out_ref[g, b, 0, mt * 2 + p] = acc[
                            b * chan : (b + 1) * chan, at : at + LANES
                        ].astype(jnp.bfloat16)


def fourier_all(cleaned, factors, n_blk, n_grp):
    n_chan = cleaned.shape[0]
    ac, as_, bc, bs = factors
    cycle_dev, _, m_width = ac.shape
    steps = RPIX // DEPTH
    rows = 2 * M_DEV // LANES
    fine = pl.BlockSpec((1, FINE, m_width), lambda c, k: (c, 0, 0))
    coarse = pl.BlockSpec((1, DEPTH // FINE, m_width), lambda c, k: (c, k, 0))
    shape = (n_grp, n_blk, cycle_dev, rows, n_chan // n_blk, LANES)
    return pl.pallas_call(
        functools.partial(fourier_kernel, n_blk, n_grp),
        grid=(cycle_dev, steps),
        out_shape=jax.ShapeDtypeStruct(shape, jnp.bfloat16),
        in_specs=[
            pl.BlockSpec((n_chan, DEPTH), lambda c, k: (0, c * steps + k)),
            fine,
            fine,
            coarse,
            coarse,
        ],
        out_specs=pl.BlockSpec(
            shape[:2] + (1,) + shape[3:], lambda c, k: (0, 0, c, 0, 0, 0)
        ),
        scratch_shapes=[
            pltpu.VMEM((DEPTH, 2 * m_width), jnp.bfloat16),
            pltpu.VMEM((n_chan, 2 * m_width), jnp.float32),
        ],
        compiler_params=pltpu.CompilerParams(vmem_limit_bytes=VMEM),
        name="fourier",
    )(cleaned, ac, as_, bc, bs)


def move_kernel(n_blk, n_grp, src_ref, dst_ref, ssem, rsem, lsem):
    blk, grp = lax.axis_index("blk"), lax.axis_index("grp")
    me = blk * n_grp + grp
    n = n_blk * n_grp
    barrier = pltpu.get_barrier_semaphore()

    def greet(s, carry):
        to = lax.rem(me + s, n)
        pl.semaphore_signal(
            barrier, inc=1, device_id=(to // n_grp, lax.rem(to, n_grp)), device_id_type=MESH
        )
        return carry

    lax.fori_loop(1, n, greet, 0)
    pl.semaphore_wait(barrier, n - 1)

    def copy_of(s):
        to = lax.rem(me + s, n)
        to_blk, to_grp = to // n_grp, lax.rem(to, n_grp)
        return pltpu.make_async_remote_copy(
            src_ref=src_ref.at[to_grp, to_blk],
            dst_ref=dst_ref.at[me],
            send_sem=ssem.at[s],
            recv_sem=rsem.at[s],
            device_id=(to_blk, to_grp),
            device_id_type=MESH,
        )

    def send(s, carry):
        copy_of(s).start()
        return carry

    lax.fori_loop(1, n, send, 0)
    own = pltpu.make_async_copy(src_ref.at[grp, blk], dst_ref.at[me], lsem)
    own.start()
    own.wait()

    def finish(s, carry):
        copy_of(s).wait_send()
        sender = lax.rem(me - s + n, n)
        pltpu.make_async_remote_copy(
            src_ref=src_ref.at[grp, blk],
            dst_ref=dst_ref.at[sender],
            send_sem=ssem.at[s],
            recv_sem=rsem.at[s],
            device_id=(sender // n_grp, lax.rem(sender, n_grp)),
            device_id_type=MESH,
        ).wait_recv()
        return carry

    lax.fori_loop(1, n, finish, 0)


def move_all(fourier, n_blk, n_grp):
    n = n_blk * n_grp
    hbm = pl.BlockSpec(memory_space=pl.ANY)
    return pl.pallas_call(
        functools.partial(move_kernel, n_blk, n_grp),
        out_shape=jax.ShapeDtypeStruct((n,) + fourier.shape[2:], jnp.bfloat16),
        in_specs=[hbm],
        out_specs=hbm,
        scratch_shapes=[
            pltpu.SemaphoreType.DMA((n,)),
            pltpu.SemaphoreType.DMA((n,)),
            pltpu.SemaphoreType.DMA,
        ],
        compiler_params=pltpu.CompilerParams(
            collective_id=1, has_side_effects=True, vmem_limit_bytes=16 * 1024 * 1024
        ),
        name="move_all",
    )(fourier)


def power_kernel(index_ref, x_ref, g_ref, mw_ref, out_ref):
    c = pl.program_id(0)
    own = index_ref[c]
    total = jnp.zeros((1, LANES), jnp.float32)
    tiles = M_DEV // LANES
    for mt in range(tiles):
        x = jnp.concatenate([x_ref[0, mt * 2], x_ref[0, mt * 2 + 1]], axis=1)
        z = jnp.dot(g_ref[own, 0], x, preferred_element_type=jnp.float32)
        z = z + jnp.dot(g_ref[own, 1], x, preferred_element_type=jnp.float32)
        sums = jnp.sum(z * x.astype(jnp.float32), axis=0, keepdims=True)
        mw = mw_ref[pl.ds(mt, 1), :]
        total = total + (sums[:, :LANES] + sums[:, LANES:]) * (mw * mw)
    out_ref[0] = jnp.broadcast_to(total, (8, LANES))


def power_of(index, x, gram, mweight):
    chan_dev, rows, n_cycle, _ = x.shape
    out = pl.pallas_call(
        power_kernel,
        grid_spec=pltpu.PrefetchScalarGridSpec(
            num_scalar_prefetch=1,
            grid=(chan_dev,),
            in_specs=[
                pl.BlockSpec((1, rows, n_cycle, LANES), lambda c, i: (c, 0, 0, 0)),
                pl.BlockSpec(gram.shape, lambda c, i: (0, 0, 0, 0)),
                pl.BlockSpec(mweight.shape, lambda c, i: (0, 0)),
            ],
            out_specs=pl.BlockSpec((1, 8, LANES), lambda c, i: (c, 0, 0)),
        ),
        out_shape=jax.ShapeDtypeStruct((chan_dev, 8, LANES), jnp.float32),
        compiler_params=pltpu.CompilerParams(vmem_limit_bytes=VMEM),
        name="power",
    )(index, x, gram, mweight)
    return jnp.sum(out[:, 0, :], axis=1)


def result_kernel(x_ref, theta_ref, w_ref, mw_ref, out_ref):
    step = pl.program_id(0)
    tiles = M_DEV // LANES
    rows = 2 * tiles
    pair = out_ref.shape[1] // rows
    lanes = w_ref.shape[1]
    shift = lax.rem(lanes - pair * step, lanes)
    part = 256
    for at in range(0, L, part):
        w = pltpu.roll(w_ref[at : at + part, :], shift, 1)
        for c in range(pair):
            own = jnp.broadcast_to(w[:, c : c + 1], (part, LANES))
            for mt in range(tiles):
                scale = own * mw_ref[mt : mt + 1, :]
                x = jnp.concatenate([x_ref[c, mt * 2], x_ref[c, mt * 2 + 1]], axis=1)
                h = jnp.dot(theta_ref[at : at + part, :], x, preferred_element_type=jnp.float32)
                row = c * rows + mt * 2
                out_ref[at : at + part, row, :] = h[:, :LANES] * scale
                out_ref[at : at + part, row + 1, :] = h[:, LANES:] * scale


def result_of(x, theta_tab, w, mweight):
    chan_dev, rows, n_cycle, _ = x.shape
    pair = 8 // rows
    full = lambda a: pl.BlockSpec(a.shape, lambda c: (0,) * a.ndim)
    return pl.pallas_call(
        result_kernel,
        grid=(chan_dev // pair,),
        out_shape=jax.ShapeDtypeStruct((L, chan_dev * rows, LANES), jnp.float32),
        in_specs=[
            pl.BlockSpec((pair, rows, n_cycle, LANES), lambda c: (c, 0, 0, 0)),
            full(theta_tab),
            full(w),
            full(mweight),
        ],
        out_specs=pl.BlockSpec((L, pair * rows, LANES), lambda c: (0, c, 0)),
        compiler_params=pltpu.CompilerParams(vmem_limit_bytes=VMEM),
        name="result",
    )(x, theta_tab, w, mweight)


def body(sky_map, fg_templates, cycle_len, beam_profile, beam_index):
    n_blk = lax.axis_size("blk")
    n_grp = lax.axis_size("grp")
    cycle_dev = cycle_len.shape[0]
    n_chan = sky_map.shape[0]
    n_mode = fg_templates.shape[1]
    chan_dev = n_chan // n_blk
    m_width = M_DEV * n_grp
    n_cycle = cycle_dev * n_blk * n_grp
    slots = jnp.arange(RPIX, dtype=jnp.int32)
    valid = (slots[None, :] < cycle_len[:, None]).reshape(-1)
    masked = jnp.where(valid[None, :], sky_map, jnp.zeros((), jnp.bfloat16))
    mode_amps = jnp.dot(fg_templates.T, masked, preferred_element_type=jnp.float32).astype(
        jnp.bfloat16
    )
    gram_part = jnp.dot(mode_amps, mode_amps.T, preferred_element_type=jnp.float32)
    cross_part = lax.dot_general(
        mode_amps, masked, (((1,), (1,)), ((), ())), preferred_element_type=jnp.float32
    )
    fill = jnp.zeros((n_mode, LANES - n_mode), jnp.float32)
    sums = sum_all(jnp.concatenate([cross_part, gram_part, fill], axis=1), n_blk, n_grp)
    lower = jnp.linalg.cholesky(sums[:, n_chan : n_chan + n_mode])
    basis = jax.scipy.linalg.solve_triangular(lower, mode_amps.astype(jnp.float32), lower=True)
    projected = jax.scipy.linalg.solve_triangular(lower, sums[:, :n_chan], lower=True)
    correction = jnp.dot(projected.T, basis, precision=lax.Precision.HIGHEST)
    cleaned = (masked.astype(jnp.float32) - correction).astype(jnp.bfloat16)
    cleaned = jnp.where(valid[None, :], cleaned, jnp.zeros((), jnp.bfloat16))
    fourier = fourier_all(cleaned, cycle_factors(cycle_len, m_width), n_blk, n_grp)
    moved = move_all(fourier, n_blk, n_grp)
    rows = fourier.shape[3]
    x = moved.reshape(n_cycle, rows, chan_dev, LANES).transpose(2, 1, 0, 3)

    theta_tab = theta_table(n_cycle)
    theta_wide = theta_tab.astype(jnp.float32)
    squared = (beam_profile * beam_profile)[:, :, None] * theta_wide[None]
    gram = jnp.einsum("plr,ls->prs", squared, theta_wide, precision=lax.Precision.HIGHEST)
    high = gram.astype(jnp.bfloat16)
    low = (gram - high.astype(jnp.float32)).astype(jnp.bfloat16)
    gram = jnp.stack([high, low], 1)
    orders = lax.axis_index("grp") * M_DEV + jnp.arange(M_DEV, dtype=jnp.int32)
    mweight = (0.25 + orders.astype(jnp.float32) / m_width).reshape(M_DEV // LANES, LANES)
    power = lax.psum(power_of(beam_index, x, gram, mweight), "grp")
    onehot = (
        beam_index[:, None] == jnp.arange(beam_profile.shape[0], dtype=jnp.int32)[None, :]
    ).astype(jnp.float32)
    profiles = jnp.dot(onehot, beam_profile, precision=lax.Precision.HIGHEST)
    scaled = profiles * lax.rsqrt(power / (2.0 * L * m_width) + 1e-06)[:, None]
    w = jnp.pad(scaled.T, ((0, 0), (0, LANES - chan_dev)))
    out = result_of(x, theta_tab, w, mweight)
    out = out.reshape(L, chan_dev, M_DEV // LANES, 2, LANES).transpose(0, 1, 3, 2, 4)
    return out.reshape(L, chan_dev, 2, M_DEV)


def solution(mesh):
    return jax.shard_map(
        body,
        mesh=mesh,
        in_specs=(P(None, ("blk", "grp")), P(), P(("blk", "grp")), P(), P("blk")),
        out_specs=P(None, "blk", None, "grp"),
        check_vma=False,
    )
```
